1024 devices in a mesh: replica: 128 (over y, z_lo, x), tensor: 8 (over z_hi, core).
Axes of the slice: x: 4, y: 4, z: 32 (z_hi: 4, z_lo: 8; z = z_hi * 8 + z_lo), core: 2. Of those that a mesh axis runs over, the one named last changes fastest.
Arguments:
- attn_out: bfloat16 [131072, 3072], P('replica', 'tensor'), may hold values from -6 to 6
- w_out: bfloat16 [3072, 4096], P('tensor'), may hold values from -0.109375 to 0.109375
- local_params: bfloat16 [128, 96, 4096], P('replica', 'tensor'), may hold values from -6 to 6
- base_params: bfloat16 [96, 4096], P('tensor'), may hold values from -6 to 6
- moment: float32 [96, 4096], P('tensor'), may hold values from -4 to 4
Outputs:
- mixed: bfloat16 [131072, 4096], P(('replica', 'tensor'))
- new_params: bfloat16 [96, 4096], P('tensor')
- new_moment: float32 [96, 4096], P('tensor')
The draws below stay inside these ranges and needn't reach their ends.
All inputs are finite; a program needn't handle non-finite values.
Results may differ from the reference program's by a relative error of at most 0.017.
Values may be sent and summed in bfloat16 or wider, within the bound.
A program may use at most 64 MiB of HBM per device.

```python
import jax
import jax.numpy as jnp
from jax import lax

D = 4096
HEADS = 24
HD = 128
TOK = 1024
TOKENS = 131072
FRAG = 96
N_REPLICA = 128
N_TENSOR = 8


def block_levels(stream_key, extent, shards, smallest, largest):
    def one(dim, shards_of):
        heights = jax.random.uniform(jax.random.fold_in(jax.random.fold_in(stream_key, 6), dim), (shards_of,), jnp.float32, smallest / len(shards), largest / len(shards))
        return jnp.repeat(jnp.exp(heights), extent[dim] // shards_of).reshape((-1,) + (1,) * (len(extent) - dim - 1))

    level = one(*shards[0])
    for cut in shards[1:]:
        level = level * one(*cut)
    return level


def bell_draw(stream_key, extent, deviation, limit, split=(), held_as=jnp.bfloat16):
    values = jax.random.normal(stream_key, extent, jnp.float32) * deviation
    if len(split) > 0:
        values = block_levels(stream_key, extent, split, -0.22, 0.18) * values
    return jnp.clip(values, min=-limit, max=limit).astype(held_as)


def setup_inputs(seed: int = 0) -> dict:
    keys = jax.random.split(jax.random.key(seed), 6)
    attn_out = bell_draw(keys[0], (TOKENS, HEADS * HD), 1.0, 6.0, ((0, 128), (1, 8)))
    w_out = bell_draw(keys[1], (HEADS * HD, D), (HEADS * HD) ** -0.5, 0.109375, ((0, 8),))
    local_params = bell_draw(keys[2], (N_REPLICA, FRAG, D), 1.0, 6.0, ((0, 128), (1, 8)))
    base_params = bell_draw(keys[3], (FRAG, D), 1.0, 6.0, ((0, 8),))
    moment = bell_draw(keys[4], (FRAG, D), 0.5, 4.0, ((0, 8),), jnp.float32)
    return dict(attn_out=attn_out, w_out=w_out, local_params=local_params, base_params=base_params, moment=moment)


outer_lr = 0.7
moment_coef = 0.9


def reference(attn_out, w_out, local_params, base_params, moment):
    group_cols = (HEADS * HD) // N_TENSOR
    attn_blocks = attn_out.reshape(N_REPLICA, TOK, HEADS * HD)

    def project(block_attn):
        def add_group(group, summed):
            part_attn = lax.dynamic_slice_in_dim(block_attn, group * group_cols, group_cols, 1)
            part_weight = lax.dynamic_slice_in_dim(w_out, group * group_cols, group_cols, 0)
            partial_value = jnp.dot(part_attn, part_weight, preferred_element_type=jnp.float32)
            rounded = lax.optimization_barrier(partial_value.astype(jnp.bfloat16))
            return summed + rounded.astype(jnp.float32)
        total = lax.fori_loop(0, N_TENSOR, add_group, jnp.zeros((TOK, D), jnp.float32))
        return total.astype(jnp.bfloat16)

    mixed = lax.map(project, attn_blocks).reshape(TOKENS, D)

    base_wide = base_params.astype(jnp.float32)

    def add_replica(replica_index, summed):
        local_rows = lax.dynamic_index_in_dim(local_params, replica_index, 0, keepdims=False)
        difference = lax.optimization_barrier((base_wide - local_rows.astype(jnp.float32)).astype(jnp.bfloat16))
        return summed + difference.astype(jnp.float32)

    summed = lax.fori_loop(0, N_REPLICA, add_replica, jnp.zeros((FRAG, D), jnp.float32))
    outer_grad = summed / N_REPLICA
    new_moment = moment_coef * moment + outer_grad
    new_params = (base_wide - outer_lr * (outer_grad + moment_coef * new_moment)).astype(jnp.bfloat16)
    return mixed, new_params, new_moment
```

```python
import jax
import jax.numpy as jnp
from jax import lax
from jax.experimental import pallas as pl
from jax.experimental.pallas import tpu as pltpu
from jax.sharding import PartitionSpec as P

MESH = pl.DeviceIdType.MESH
outer_lr = 0.7
moment_coef = 0.9

PIECES = 8
ROWS = 48
COLS = 256
BLOCKS = 16
OFFSETS = (0, -1, 1, 2)
ROUNDS = PIECES + 3


def kernel(
    attn, w, local_params, base, moment, out, new_params, new_moment,
    wall, own, heads, relay, acc, give, take, diff, diffs, zsum, ztake, grad,
    local_sem, first_send, first_recv, win_send, win_recv, plane_send, plane_recv,
    attn_send, attn_recv, diff_send, diff_recv, z_send, z_recv, grad_send, grad_recv, half_send, half_recv,
):
    replica, tensor = lax.axis_index("replica"), lax.axis_index("tensor")
    x, z_lo, y = lax.rem(replica, 4), lax.rem(lax.div(replica, 4), 8), lax.div(replica, 32)
    z_hi, core = lax.div(tensor, 2), lax.rem(tensor, 2)
    z = z_hi * 8 + z_lo
    mine = y * 4 + x

    def device(x, y, z, core):
        x, y, z = lax.rem(x + 8, 4), lax.rem(y + 8, 4), lax.rem(z + 64, 32)
        return {
            "replica": (y * 8 + lax.rem(z, 8)) * 4 + x,
            "tensor": lax.div(z, 8) * 2 + core,
        }

    def copy(source, target, send, recv, to):
        return pltpu.make_async_remote_copy(
            src_ref=source, dst_ref=target, send_sem=send, recv_sem=recv, device_id=to, device_id_type=MESH
        )

    columns = pl.ds(pl.multiple_of(mine * COLS, COLS), COLS)
    locals_ = [
        pltpu.make_async_copy(w.at[:, :, columns], wall.at[mine, :, 0], local_sem.at[0]),
        pltpu.make_async_copy(w.at[:, :, columns], wall.at[mine, :, 4], local_sem.at[1]),
        pltpu.make_async_copy(w, own, local_sem.at[2]),
        pltpu.make_async_copy(attn.at[pl.ds(pl.multiple_of(z_hi * 256, 256), 256)], heads.at[0], local_sem.at[3]),
    ]
    for one in locals_:
        one.start()

    def z_partner(step):
        bit = 1 << step
        return z + bit - 2 * bit * lax.rem(lax.div(z_lo, bit), 2)

    partners = [device(x + j % 4, y + j // 4, z, core) for j in range(1, 16)]
    partners += [device(x, y, z + 1, core), device(x, y, z - 1, core)]
    partners += [device(x, y, z + 8 * j, core) for j in (1, 2, 3)]
    partners += [device(x, y, z_partner(step), core) for step in (1, 2)]
    sibling = device(x, y, z, 1 - core)
    partners += [sibling]
    barrier = pltpu.get_barrier_semaphore()
    for one in partners:
        pl.semaphore_signal(barrier, inc=1, device_id=one, device_id_type=MESH)

    diff[...] = jnp.zeros_like(diff)

    @pl.loop(0, BLOCKS)
    def _(block):
        at = pl.ds(pl.multiple_of(block * COLS, COLS), COLS)
        wide = base[:, at].astype(jnp.float32) - local_params[:, at].astype(jnp.float32)
        diff[block, 0:12, :] = wide.astype(jnp.bfloat16)

    locals_[0].wait()
    locals_[1].wait()
    pl.semaphore_wait(barrier, len(partners))

    firsts = []
    for j in (1, 2, 3):
        firsts.append(
            copy(
                wall.at[mine, z_lo, 0], wall.at[mine, z_lo, 4 - j],
                first_send.at[j - 1], first_recv.at[3 - j], device(x, y, z + 8 * j, core),
            )
        )
        firsts[-1].start()

    diff_copies = []
    for j in range(1, 16):
        dx, dy = j % 4, j // 4
        block = lax.rem(y + dy, 4) * 4 + lax.rem(x + dx, 4)
        diff_copies.append(
            copy(
                diff.at[block], diffs.at[j - 1], diff_send.at[j - 1], diff_recv.at[j - 1],
                device(x + dx, y + dy, z, core),
            )
        )
        diff_copies[-1].start()

    def rows_of(j, start, size):
        return attn.at[pl.ds(pl.multiple_of(lax.rem(z_hi + j, 4) * 256 + start, 128), size)]

    up, down = device(x, y, z + 8, core), device(x, y, z - 8, core)
    attn_copies = [
        copy(rows_of(2, 0, 128), relay.at[0], attn_send.at[0], attn_recv.at[0], up),
        copy(rows_of(2, 128, 128), relay.at[1], attn_send.at[1], attn_recv.at[1], down),
        copy(rows_of(1, 0, 256), heads.at[3], attn_send.at[2], attn_recv.at[2], up),
        copy(rows_of(3, 0, 256), heads.at[1], attn_send.at[3], attn_recv.at[3], down),
    ]
    for one in attn_copies:
        one.start()
    relays = [
        copy(relay.at[0], heads.at[2, pl.ds(0, 128)], attn_send.at[4], attn_recv.at[4], up),
        copy(relay.at[1], heads.at[2, pl.ds(128, 128)], attn_send.at[5], attn_recv.at[5], down),
    ]

    def piece_of(n):
        away = lax.div(n + 1, 2)
        return lax.rem(z_lo + jnp.where(lax.rem(n, 2) == 1, 8 - away, away), 8)

    def window(piece, n, upward):
        if upward:
            start, to = 1 + lax.div(z_lo, 7), device(x, y, z + 1, core)
        else:
            start, to = 1 - lax.div(7 - z_lo, 7), device(x, y, z - 1, core)
        return copy(
            wall.at[mine, piece, pl.ds(start, 3)], wall.at[mine, piece, pl.ds(1, 3)],
            win_send.at[n - 1], win_recv.at[n - 1], to,
        )

    def plane(n, piece, a, b, to_a, to_b, which):
        first_x = 1 - lax.rem(n, 2)
        sx, sy = a * first_x + b * (1 - first_x), b * first_x + a * (1 - first_x)
        tx, ty = to_a * first_x + to_b * (1 - first_x), to_b * first_x + to_a * (1 - first_x)
        block = lax.rem(y + sy + 4, 4) * 4 + lax.rem(x + sx + 4, 4)
        part = wall.at[block, piece, pl.ds(1, 3)]
        index = n * 15 + which
        return copy(part, part, plane_send.at[index], plane_recv.at[index], device(x + tx, y + ty, z, core))

    def spread(n, piece, i):
        plane(n, piece, OFFSETS[i], 0, 0, 1, 3 + 3 * i).start()
        plane(n, piece, OFFSETS[i], 0, 0, -1, 4 + 3 * i).start()

    def arrive(n, which):
        part = wall.at[mine, 0, pl.ds(1, 3)]
        index = n * 15 + which
        copy(part, part, plane_send.at[index], plane_recv.at[index], sibling).wait_recv()

    def stage0(n):
        piece = piece_of(n)

        @pl.when(n >= 1)
        def _():
            window(piece, n, True).wait_recv()

        @pl.when(n == 0)
        def _():
            window(piece, n + 1, True).start()

        @pl.when(n <= 5)
        def _():
            @pl.when(lax.rem(n, 2) == 1)
            def _():
                window(piece, n + 2, True).start()

            @pl.when(lax.rem(n, 2) == 0)
            def _():
                window(piece, n + 2, False).start()

        plane(n, piece, 0, 0, 1, 0, 0).start()
        plane(n, piece, 0, 0, -1, 0, 1).start()
        spread(n, piece, 0)

    def stage1(n):
        piece = piece_of(n)
        route = lax.rem(lax.div(n, 2), 2)
        arrive(n, 0)

        @pl.when(route == 0)
        def _():
            plane(n, piece, -1, 0, 1, 0, 2).start()

        spread(n, piece, 1)
        arrive(n, 1)

        @pl.when(route == 1)
        def _():
            plane(n, piece, 1, 0, -1, 0, 2).start()

        spread(n, piece, 2)

    def stage2(n):
        piece = piece_of(n)
        arrive(n, 2)
        spread(n, piece, 3)

    def stage3(n):
        piece = piece_of(n)
        for i in range(4):
            arrive(n, 3 + 3 * i)
            if i % 2 == 0:
                plane(n, piece, OFFSETS[i], -1, 0, 1, 5 + 3 * i).start()
            arrive(n, 4 + 3 * i)
            if i % 2 == 1:
                plane(n, piece, OFFSETS[i], 1, 0, -1, 5 + 3 * i).start()

    for one in firsts:
        one.wait_recv()

    z_copies = [
        copy(zsum.at[step], ztake.at[step], z_send.at[step], z_recv.at[step], device(x, y, z_partner(step), core))
        for step in range(3)
    ]
    grad_copies = []
    for j in range(1, 16):
        grad_copies.append(
            copy(
                zsum.at[3], grad.at[mine], grad_send.at[j - 1], grad_recv.at[j - 1],
                device(x + j % 4, y + j // 4, z, core),
            )
        )

    @pl.loop(0, ROUNDS)
    def _(m):
        @pl.when(m < PIECES)
        def _():
            stage0(m)

        @pl.when((m >= 1) & (m < PIECES + 1))
        def _():
            stage1(m - 1)

        @pl.when((m >= 2) & (m < PIECES + 2))
        def _():
            stage2(m - 2)

        @pl.when(m >= 3)
        def _():
            stage3(m - 3)

        @pl.when(m == 1)
        def _():
            for one in diff_copies:
                one.wait_recv()
            total = diff[mine].astype(jnp.float32)
            for j in range(15):
                total = total + diffs[j].astype(jnp.float32)
            zsum[0] = total
            z_copies[0].start()

        for step in range(3):

            @pl.when(m == 2 + step)
            def _(step=step):
                z_copies[step].wait_recv()
                zsum[step + 1] = zsum[step] + ztake[step]
                if step < 2:
                    z_copies[step + 1].start()
                else:
                    grad[mine] = zsum[3]
                    for one in grad_copies:
                        one.start()

        @pl.when(m == 3)
        def _():
            for index in (0, 1):
                attn_copies[index].wait_recv()
                relays[index].start()

    @pl.loop(0, PIECES)
    def _(n):
        for i in range(4):
            arrive(n, 5 + 3 * i)

    for one in grad_copies:
        one.wait_recv()

    @pl.loop(0, BLOCKS)
    def _(block):
        at = pl.ds(pl.multiple_of(block * COLS, COLS), COLS)
        outer_grad = grad[block, 0:12, :] / 128
        moved = moment_coef * moment[:, at] + outer_grad
        new_moment[:, at] = moved
        new_params[:, at] = (
            base[:, at].astype(jnp.float32) - outer_lr * (outer_grad + moment_coef * moved)
        ).astype(jnp.bfloat16)

    def part(index, block):
        return jnp.dot(
            heads[index], wall[block, :, index].reshape(PIECES * ROWS, COLS), preferred_element_type=jnp.float32
        )

    locals_[2].wait()
    locals_[3].wait()

    @pl.loop(0, BLOCKS)
    def _(block):
        at = pl.ds(pl.multiple_of(block * COLS, COLS), COLS)
        acc[block] = jnp.dot(
            heads[0], own[:, :, at].reshape(PIECES * ROWS, COLS), preferred_element_type=jnp.float32
        )

    attn_copies[2].wait_recv()
    attn_copies[3].wait_recv()

    @pl.loop(0, BLOCKS)
    def _(block):
        acc[block] += part(1, block) + part(3, block)

    relays[0].wait_recv()
    relays[1].wait_recv()
    kept = pl.ds(pl.multiple_of(core * 128, 128), 128)
    given = pl.ds(pl.multiple_of((1 - core) * 128, 128), 128)

    def half(block):
        return copy(give.at[block], take.at[block], half_send.at[block], half_recv.at[block], sibling)

    @pl.loop(0, BLOCKS)
    def _(block):
        acc[block] += part(2, block)
        give[block] = acc[block, given, :].astype(jnp.bfloat16)
        half(block).start()

    @pl.loop(0, BLOCKS)
    def _(block):
        at = pl.ds(pl.multiple_of(block * COLS, COLS), COLS)
        half(block).wait_recv()
        out[:, at] = (acc[block, kept, :] + take[block].astype(jnp.float32)).astype(jnp.bfloat16)

    @pl.loop(0, PIECES * 15)
    def _(index):
        part_ = wall.at[mine, 0, pl.ds(1, 3)]
        copy(part_, part_, plane_send.at[index], plane_recv.at[index], sibling).wait_send()

    @pl.loop(0, BLOCKS)
    def _(block):
        half(block).wait_send()

    for n in range(1, 8):
        window(0, n, True).wait_send()
    for one in firsts + diff_copies + attn_copies + relays + z_copies + grad_copies:
        one.wait_send()


def local(attn_out, w_out, local_params, base_params, moment):
    vmem, hbm = pl.BlockSpec(memory_space=pltpu.VMEM), pl.BlockSpec(memory_space=pl.ANY)
    dma = pltpu.SemaphoreType.DMA
    bf16, f32 = jnp.bfloat16, jnp.float32
    return pl.pallas_call(
        kernel,
        out_shape=(
            jax.ShapeDtypeStruct((128, 4096), bf16),
            jax.ShapeDtypeStruct((12, 4096), bf16),
            jax.ShapeDtypeStruct((12, 4096), f32),
        ),
        in_specs=[hbm, hbm, vmem, vmem, vmem],
        out_specs=(vmem, vmem, vmem),
        scratch_shapes=[
            pltpu.VMEM((BLOCKS, PIECES, 5, ROWS, COLS), bf16),
            pltpu.VMEM((PIECES, ROWS, 4096), bf16),
            pltpu.VMEM((4, 256, 384), bf16),
            pltpu.VMEM((2, 128, 384), bf16),
            pltpu.VMEM((BLOCKS, 256, COLS), f32),
            pltpu.VMEM((BLOCKS, 128, COLS), bf16),
            pltpu.VMEM((BLOCKS, 128, COLS), bf16),
            pltpu.VMEM((BLOCKS, 16, COLS), bf16),
            pltpu.VMEM((15, 16, COLS), bf16),
            pltpu.VMEM((4, 16, COLS), f32),
            pltpu.VMEM((3, 16, COLS), f32),
            pltpu.VMEM((BLOCKS, 16, COLS), f32),
            dma((4,)),
            dma((3,)),
            dma((3,)),
            dma((7,)),
            dma((7,)),
            dma((PIECES * 15,)),
            dma((PIECES * 15,)),
            dma((6,)),
            dma((6,)),
            dma((15,)),
            dma((15,)),
            dma((3,)),
            dma((3,)),
            dma((15,)),
            dma((15,)),
            dma((BLOCKS,)),
            dma((BLOCKS,)),
        ],
        compiler_params=pltpu.CompilerParams(
            collective_id=0, has_side_effects=True, vmem_limit_bytes=56 * 1024 * 1024
        ),
        cost_estimate=pl.CostEstimate(flops=2 * 256 * 1536 * 4096, bytes_accessed=8 << 20, transcendentals=0),
    )(attn_out, w_out.reshape(PIECES, ROWS, 4096), local_params.reshape(12, 4096), base_params, moment)


def solution(mesh):
    in_specs = (
        P("replica", "tensor"),
        P("tensor", None),
        P("replica", "tensor", None),
        P("tensor", None),
        P("tensor", None),
    )
    out_specs = (P(("replica", "tensor"), None), P("tensor", None), P("tensor", None))
    return jax.shard_map(local, mesh=mesh, in_specs=in_specs, out_specs=out_specs, check_vma=False)
```

```python
import jax
import jax.numpy as jnp
from jax import lax
from jax.experimental import pallas as pl
from jax.experimental.pallas import tpu as pltpu
from jax.sharding import PartitionSpec as P

MESH = pl.DeviceIdType.MESH
outer_lr = 0.7
moment_coef = 0.9

PIECES = 8
ROWS = 48
COLS = 256
BLOCKS = 16
OFFSETS = (0, -1, 1, 2)
ROUNDS = PIECES + 2
FAR_STEPS = (0, 1, 2, 3)
NEAR_STEPS = (5, 6, 7, 8)
UNROLL = 1
RELAY_ROUNDS = (0, 1, 2, 3)
PARTS = len(FAR_STEPS)


def kernel(
    attn, w, local_params, base, out, summed,
    wall, own, heads, relay, acc, give, take, diff, diffs, zsum, ztake, grad,
    local_sem, first_send, first_recv, win_send, win_recv, plane_send, plane_recv,
    near_send, near_recv, far_send, far_recv, relay_send, relay_recv, diff_send, diff_recv, z_send, z_recv, grad_send, grad_recv, half_send, half_recv,
):
    replica, tensor = lax.axis_index("replica"), lax.axis_index("tensor")
    x, z_lo, y = lax.rem(replica, 4), lax.rem(lax.div(replica, 4), 8), lax.div(replica, 32)
    z_hi, core = lax.div(tensor, 2), lax.rem(tensor, 2)
    z = z_hi * 8 + z_lo
    mine = y * 4 + x

    def device(x, y, z, core):
        x, y, z = lax.rem(x + 8, 4), lax.rem(y + 8, 4), lax.rem(z + 64, 32)
        return {
            "replica": (y * 8 + lax.rem(z, 8)) * 4 + x,
            "tensor": lax.div(z, 8) * 2 + core,
        }

    def copy(source, target, send, recv, to):
        return pltpu.make_async_remote_copy(
            src_ref=source, dst_ref=target, send_sem=send, recv_sem=recv, device_id=to, device_id_type=MESH
        )

    columns = pl.ds(pl.multiple_of(mine * COLS, COLS), COLS)
    locals_ = [
        pltpu.make_async_copy(w.at[:, :, columns], wall.at[mine, :, 0], local_sem.at[0]),
        pltpu.make_async_copy(w.at[:, :, columns], wall.at[mine, :, 4], local_sem.at[1]),
        pltpu.make_async_copy(w, own, local_sem.at[2]),
        pltpu.make_async_copy(attn.at[pl.ds(pl.multiple_of(z_hi * 256, 256), 256)], heads.at[0], local_sem.at[3]),
    ]
    for one in locals_:
        one.start()

    def z_partner(step):
        bit = 1 << step
        return z + bit - 2 * bit * lax.rem(lax.div(z_lo, bit), 2)

    partners = [device(x + j % 4, y + j // 4, z, core) for j in range(1, 16)]
    partners += [device(x, y, z + 1, core), device(x, y, z - 1, core)]
    partners += [device(x, y, z + 8 * j, core) for j in (1, 2, 3)]
    partners += [device(x, y, z_partner(step), core) for step in (1, 2)]
    sibling = device(x, y, z, 1 - core)
    partners += [sibling]
    barrier = pltpu.get_barrier_semaphore()
    for one in partners:
        pl.semaphore_signal(barrier, inc=1, device_id=one, device_id_type=MESH)

    pl.semaphore_wait(barrier, len(partners))

    firsts = []
    for j in (1, 2, 3):
        firsts.append(
            copy(
                w.at[z_lo, :, columns], wall.at[mine, z_lo, 4 - j],
                first_send.at[j - 1], first_recv.at[3 - j], device(x, y, z + 8 * j, core),
            )
        )
        firsts[-1].start()

    diff[...] = jnp.zeros_like(diff)

    @pl.loop(0, BLOCKS)
    def _(block):
        at = pl.ds(pl.multiple_of(block * COLS, COLS), COLS)
        wide = base[:, at].astype(jnp.float32) - local_params[:, at].astype(jnp.float32)
        diff[block, 0:12, :] = wide.astype(jnp.bfloat16)

    diff_copies = []
    for j in range(1, 16):
        dx, dy = j % 4, j // 4
        block = lax.rem(y + dy, 4) * 4 + lax.rem(x + dx, 4)
        diff_copies.append(
            copy(
                diff.at[block], diffs.at[j - 1], diff_send.at[j - 1], diff_recv.at[j - 1],
                device(x + dx, y + dy, z, core),
            )
        )
        diff_copies[-1].start()

    def rows_of(j, start, size):
        return attn.at[pl.ds(pl.multiple_of(lax.rem(z_hi + j, 4) * 256 + start, 16), size)]

    up, down = device(x, y, z + 8, core), device(x, y, z - 8, core)
    high = 128 // PARTS
    far_copies, relays = [], []
    for k in range(PARTS):
        for side, to in enumerate((up, down)):
            held = relay.at[side, pl.ds(k * high, high)]
            landing = heads.at[2, pl.ds(side * 128 + k * high, high)]
            index = 2 * k + side
            far_copies.append(
                copy(rows_of(2, side * 128 + k * high, high), held, far_send.at[index], far_recv.at[index], to)
            )
            relays.append(copy(held, landing, relay_send.at[index], relay_recv.at[index], to))
    near_copies = []
    for k in range(PARTS):
        part_rows = pl.ds(k * 64, 64)
        near_copies += [
            copy(rows_of(1, k * 64, 64), heads.at[3, part_rows], near_send.at[2 * k], near_recv.at[2 * k], up),
            copy(rows_of(3, k * 64, 64), heads.at[1, part_rows], near_send.at[2 * k + 1], near_recv.at[2 * k + 1], down),
        ]

    def piece_of(n):
        away = (n + 1) // 2
        odd = n % 2
        return lax.rem(z_lo + odd * (8 - away) + (1 - odd) * away, 8)

    def window(piece, n, upward):
        if upward:
            start, to = 1 + lax.div(z_lo, 7), device(x, y, z + 1, core)
        else:
            start, to = 1 - lax.div(7 - z_lo, 7), device(x, y, z - 1, core)
        return copy(
            wall.at[mine, piece, pl.ds(start, 3)], wall.at[mine, piece, pl.ds(1, 3)],
            win_send.at[n - 1], win_recv.at[n - 1], to,
        )

    def plane(n, piece, a, b, to_a, to_b, which):
        first_x = 1 - n % 2
        sx, sy = a * first_x + b * (1 - first_x), b * first_x + a * (1 - first_x)
        tx, ty = to_a * first_x + to_b * (1 - first_x), to_b * first_x + to_a * (1 - first_x)
        block = lax.rem(y + sy + 4, 4) * 4 + lax.rem(x + sx + 4, 4)
        part = wall.at[block, piece, pl.ds(1, 3)]
        index = n * 15 + which
        return copy(part, part, plane_send.at[index], plane_recv.at[index], device(x + tx, y + ty, z, core))

    def spread(n, piece, i):
        plane(n, piece, OFFSETS[i], 0, 0, 1, 3 + 3 * i).start()
        plane(n, piece, OFFSETS[i], 0, 0, -1, 4 + 3 * i).start()

    def arrive(n, which):
        part = wall.at[mine, 0, pl.ds(1, 3)]
        index = n * 15 + which
        copy(part, part, plane_send.at[index], plane_recv.at[index], sibling).wait_recv()

    def window_take(n, upward):
        piece = piece_of(n)
        window(piece, n, upward).wait_recv()

        if n + 2 < PIECES:
            window(piece, n + 2, upward).start()

        stage0(n)

    def stage0(n):
        piece = piece_of(n)
        plane(n, piece, 0, 0, 1, 0, 0).start()
        plane(n, piece, 0, 0, -1, 0, 1).start()
        spread(n, piece, 0)

    def stage1(n):
        piece = piece_of(n)
        route = lax.rem(lax.div(n, 2), 2)
        arrive(n, 0)

        @pl.when(route == 0)
        def _():
            plane(n, piece, -1, 0, 1, 0, 2).start()

        spread(n, piece, 1)
        arrive(n, 1)

        @pl.when(route == 1)
        def _():
            plane(n, piece, 1, 0, -1, 0, 2).start()

        spread(n, piece, 2)

    def stage2(n):
        piece = piece_of(n)
        arrive(n, 2)
        spread(n, piece, 3)

    def stage3(n, i):
        piece = piece_of(n)
        arrive(n, 3 + 3 * i)
        if i % 2 == 0:
            plane(n, piece, OFFSETS[i], -1, 0, 1, 5 + 3 * i).start()
        arrive(n, 4 + 3 * i)
        if i % 2 == 1:
            plane(n, piece, OFFSETS[i], 1, 0, -1, 5 + 3 * i).start()

    z_copies = [
        copy(zsum.at[step], ztake.at[step], z_send.at[step], z_recv.at[step], device(x, y, z_partner(step), core))
        for step in range(3)
    ]
    grad_copies = []
    for j in range(1, 16):
        grad_copies.append(
            copy(
                zsum.at[3], grad.at[mine], grad_send.at[j - 1], grad_recv.at[j - 1],
                device(x + j % 4, y + j // 4, z, core),
            )
        )

    def attn_step(m):
        for k in range(PARTS):
            if m == FAR_STEPS[k]:
                far_copies[2 * k].start()
                far_copies[2 * k + 1].start()
        for k in range(PARTS):
            if m == NEAR_STEPS[k]:
                near_copies[2 * k].start()
                near_copies[2 * k + 1].start()

    def sum_step(step):
        z_copies[step].wait_recv()
        zsum[step + 1] = zsum[step] + ztake[step]
        if step < 2:
            z_copies[step + 1].start()
        else:
            grad[mine] = zsum[3]
            for one in grad_copies:
                one.start()

    attn_step(0)
    for one in diff_copies:
        one.wait_recv()
    total = diff[mine].astype(jnp.float32)
    for j in range(15):
        total = total + diffs[j].astype(jnp.float32)
    zsum[0] = total
    z_copies[0].start()
    sum_step(0)
    locals_[0].wait()
    locals_[1].wait()
    for one in firsts:
        one.wait_recv()
    window(z_lo, 1, True).start()
    window(z_lo, 2, False).start()
    stage0(0)
    sum_step(1)
    attn_step(1)
    locals_[2].wait()
    locals_[3].wait()

    @pl.loop(0, BLOCKS, unroll=UNROLL)
    def _(block):
        at = pl.ds(pl.multiple_of(block * COLS, COLS), COLS)
        acc[block] = jnp.dot(
            heads[0], own[:, :, at].reshape(PIECES * ROWS, COLS), preferred_element_type=jnp.float32
        )

    for step in range(3):
        window_take(2 * step + 1, True)
        window_take(2 * step + 2, False)
        if step == 0:
            sum_step(2)
        attn_step(2 + step)
    window_take(7, True)
    attn_step(5)

    @pl.loop(0, ROUNDS)
    def _(m):
        @pl.when(m < PIECES)
        def _():
            stage1(m)
            stage3(m, 0)

        @pl.when((m >= 1) & (m < PIECES + 1))
        def _():
            stage2(m - 1)
            stage3(m - 1, 1)
            stage3(m - 1, 2)

        @pl.when(m >= 2)
        def _():
            stage3(m - 2, 3)

        for k in range(PARTS):
            if NEAR_STEPS[k] >= 6:

                @pl.when(m == NEAR_STEPS[k] - 6)
                def _(k=k):
                    near_copies[2 * k].start()
                    near_copies[2 * k + 1].start()

            @pl.when(m == RELAY_ROUNDS[k])
            def _(k=k):
                for index in (2 * k, 2 * k + 1):
                    far_copies[index].wait_recv()
                    relays[index].start()

    @pl.loop(0, PIECES)
    def _(n):
        for i in range(4):
            arrive(n, 5 + 3 * i)

    for one in grad_copies:
        one.wait_recv()

    @pl.loop(0, BLOCKS)
    def _(block):
        at = pl.ds(pl.multiple_of(block * COLS, COLS), COLS)
        summed[:, at] = grad[block, 0:12, :]

    def part(index, block):
        return jnp.dot(
            heads[index], wall[block, :, index].reshape(PIECES * ROWS, COLS), preferred_element_type=jnp.float32
        )

    for one in near_copies:
        one.wait_recv()

    @pl.loop(0, BLOCKS, unroll=UNROLL)
    def _(block):
        acc[block] += part(1, block) + part(3, block)

    for one in relays:
        one.wait_recv()
    kept = pl.ds(pl.multiple_of(core * 128, 128), 128)
    given = pl.ds(pl.multiple_of((1 - core) * 128, 128), 128)

    def half(block):
        return copy(give.at[block], take.at[block], half_send.at[block], half_recv.at[block], sibling)

    @pl.loop(0, BLOCKS, unroll=UNROLL)
    def _(block):
        acc[block] += part(2, block)
        give[block] = acc[block, given, :].astype(jnp.bfloat16)
        half(block).start()

    @pl.loop(0, BLOCKS, unroll=UNROLL)
    def _(block):
        at = pl.ds(pl.multiple_of(block * COLS, COLS), COLS)
        half(block).wait_recv()
        out[:, at] = (acc[block, kept, :] + take[block].astype(jnp.float32)).astype(jnp.bfloat16)

    @pl.loop(0, PIECES * 15)
    def _(index):
        part_ = wall.at[mine, 0, pl.ds(1, 3)]
        copy(part_, part_, plane_send.at[index], plane_recv.at[index], sibling).wait_send()

    @pl.loop(0, BLOCKS)
    def _(block):
        half(block).wait_send()

    for n in range(1, 8):
        window(0, n, True).wait_send()
    for one in firsts + diff_copies + near_copies + far_copies + relays + z_copies + grad_copies:
        one.wait_send()


def local(attn_out, w_out, local_params, base_params, moment):
    vmem, hbm = pl.BlockSpec(memory_space=pltpu.VMEM), pl.BlockSpec(memory_space=pl.ANY)
    dma = pltpu.SemaphoreType.DMA
    bf16, f32 = jnp.bfloat16, jnp.float32
    projected, summed = pl.pallas_call(
        kernel,
        out_shape=(jax.ShapeDtypeStruct((128, 4096), bf16), jax.ShapeDtypeStruct((12, 4096), f32)),
        in_specs=[hbm, hbm, vmem, vmem],
        out_specs=(vmem, vmem),
        scratch_shapes=[
            pltpu.VMEM((BLOCKS, PIECES, 5, ROWS, COLS), bf16),
            pltpu.VMEM((PIECES, ROWS, 4096), bf16),
            pltpu.VMEM((4, 256, 384), bf16),
            pltpu.VMEM((2, 128, 384), bf16),
            pltpu.VMEM((BLOCKS, 256, COLS), f32),
            pltpu.VMEM((BLOCKS, 128, COLS), bf16),
            pltpu.VMEM((BLOCKS, 128, COLS), bf16),
            pltpu.VMEM((BLOCKS, 16, COLS), bf16),
            pltpu.VMEM((15, 16, COLS), bf16),
            pltpu.VMEM((4, 16, COLS), f32),
            pltpu.VMEM((3, 16, COLS), f32),
            pltpu.VMEM((BLOCKS, 16, COLS), f32),
            dma((4,)),
            dma((3,)),
            dma((3,)),
            dma((7,)),
            dma((7,)),
            dma((PIECES * 15,)),
            dma((PIECES * 15,)),
            dma((2 * PARTS,)),
            dma((2 * PARTS,)),
            dma((2 * PARTS,)),
            dma((2 * PARTS,)),
            dma((2 * PARTS,)),
            dma((2 * PARTS,)),
            dma((15,)),
            dma((15,)),
            dma((3,)),
            dma((3,)),
            dma((15,)),
            dma((15,)),
            dma((BLOCKS,)),
            dma((BLOCKS,)),
        ],
        compiler_params=pltpu.CompilerParams(
            collective_id=0, has_side_effects=True, vmem_limit_bytes=56 * 1024 * 1024
        ),
        cost_estimate=pl.CostEstimate(flops=2 * 256 * 1536 * 4096, bytes_accessed=8 << 20, transcendentals=0),
    )(attn_out, w_out.reshape(PIECES, ROWS, 4096), local_params.reshape(12, 4096), base_params)
    outer_grad = summed / lax.axis_size("replica")
    new_moment = moment_coef * moment + outer_grad
    new_params = (base_params.astype(f32) - outer_lr * (outer_grad + moment_coef * new_moment)).astype(bf16)
    return projected, new_params, new_moment


def solution(mesh):
    in_specs = (
        P("replica", "tensor"),
        P("tensor", None),
        P("replica", "tensor", None),
        P("tensor", None),
        P("tensor", None),
    )
    out_specs = (P(("replica", "tensor"), None), P("tensor", None), P("tensor", None))
    return jax.shard_map(local, mesh=mesh, in_specs=in_specs, out_specs=out_specs, check_vma=False)
```

```python
import jax
import jax.numpy as jnp
from jax import lax
from jax.experimental import pallas as pl
from jax.experimental.pallas import tpu as pltpu
from jax.sharding import PartitionSpec as P

MESH = pl.DeviceIdType.MESH
outer_lr = 0.7
moment_coef = 0.9

PIECES = 8
ROWS = 48
COLS = 256
BLOCKS = 16
OFFSETS = (0, -1, 1, 2)
ROUNDS = PIECES + 2
FAR_STEPS = (0, 1, 2, 3)
NEAR_STEPS = (4, 6, 7, 8)
UNROLL = 1
RELAY_ROUNDS = (1, 2, 3, 4)
PARTS = len(FAR_STEPS)


def kernel(
    attn, w, local_hbm, base_hbm, out, summed, local_params, base,
    wall, own, heads, relay, acc, give, take, diff, diffs, zsum, ztake, grad,
    local_sem, first_send, first_recv, win_send, win_recv, plane_send, plane_recv,
    near_send, near_recv, far_send, far_recv, relay_send, relay_recv, diff_send, diff_recv, z_send, z_recv, grad_send, grad_recv, half_send, half_recv,
):
    replica, tensor = lax.axis_index("replica"), lax.axis_index("tensor")
    x, z_lo, y = lax.rem(replica, 4), lax.rem(lax.div(replica, 4), 8), lax.div(replica, 32)
    z_hi, core = lax.div(tensor, 2), lax.rem(tensor, 2)
    z = z_hi * 8 + z_lo
    mine = y * 4 + x

    def device(x, y, z, core):
        x, y, z = lax.rem(x + 8, 4), lax.rem(y + 8, 4), lax.rem(z + 64, 32)
        return {
            "replica": (y * 8 + lax.rem(z, 8)) * 4 + x,
            "tensor": lax.div(z, 8) * 2 + core,
        }

    def copy(source, target, send, recv, to):
        return pltpu.make_async_remote_copy(
            src_ref=source, dst_ref=target, send_sem=send, recv_sem=recv, device_id=to, device_id_type=MESH
        )

    columns = pl.ds(pl.multiple_of(mine * COLS, COLS), COLS)
    locals_ = [
        pltpu.make_async_copy(w.at[:, :, columns], wall.at[mine, :, 0], local_sem.at[0]),
        pltpu.make_async_copy(w.at[:, :, columns], wall.at[mine, :, 4], local_sem.at[1]),
        pltpu.make_async_copy(w, own, local_sem.at[2]),
        pltpu.make_async_copy(attn.at[pl.ds(pl.multiple_of(z_hi * 256, 256), 256)], heads.at[0], local_sem.at[3]),
        pltpu.make_async_copy(local_hbm, local_params, local_sem.at[4]),
        pltpu.make_async_copy(base_hbm, base, local_sem.at[5]),
    ]
    for one in locals_:
        one.start()

    def z_partner(step):
        bit = 1 << step
        return z + bit - 2 * bit * lax.rem(lax.div(z_lo, bit), 2)

    partners = [device(x + j % 4, y + j // 4, z, core) for j in range(1, 16)]
    partners += [device(x, y, z + 1, core), device(x, y, z - 1, core)]
    partners += [device(x, y, z + 8, core), device(x, y, z - 8, core)]
    partners += [device(x, y, z_partner(step), core) for step in (1, 2)]
    sibling = device(x, y, z, 1 - core)
    partners += [sibling]
    barrier = pltpu.get_barrier_semaphore()
    for one in partners:
        pl.semaphore_signal(barrier, inc=1, device_id=one, device_id_type=MESH)

    pl.semaphore_wait(barrier, len(partners))

    firsts = [
        copy(
            w.at[z_lo, :, columns], wall.at[mine, z_lo, 4 - j], first_send.at[j - 1], first_recv.at[j - 1],
            device(x, y, z + 8 * j, core),
        )
        for j in (1, 3)
    ]
    for one in firsts:
        one.start()
    second = copy(
        wall.at[mine, z_lo, 1 + 2 * core], wall.at[mine, z_lo, 2], first_send.at[1], first_recv.at[1],
        device(x, y, z - 8 + 16 * core, core),
    )

    diff[...] = jnp.zeros_like(diff)
    locals_[4].wait()
    locals_[5].wait()

    @pl.loop(0, BLOCKS)
    def _(block):
        at = pl.ds(pl.multiple_of(block * COLS, COLS), COLS)
        wide = base[:, at].astype(jnp.float32) - local_params[:, at].astype(jnp.float32)
        diff[block, 0:12, :] = wide.astype(jnp.bfloat16)

    diff_copies = []
    for j in range(1, 16):
        dx, dy = j % 4, j // 4
        block = lax.rem(y + dy, 4) * 4 + lax.rem(x + dx, 4)
        diff_copies.append(
            copy(
                diff.at[block], diffs.at[j - 1], diff_send.at[j - 1], diff_recv.at[j - 1],
                device(x + dx, y + dy, z, core),
            )
        )
        diff_copies[-1].start()

    def rows_of(j, start, size):
        return attn.at[pl.ds(pl.multiple_of(lax.rem(z_hi + j, 4) * 256 + start, 16), size)]

    up, down = device(x, y, z + 8, core), device(x, y, z - 8, core)
    high = 128 // PARTS
    far_copies, relays = [], []
    for k in range(PARTS):
        for side, to in enumerate((up, down)):
            held = relay.at[side, pl.ds(k * high, high)]
            landing = heads.at[2, pl.ds(side * 128 + k * high, high)]
            index = 2 * k + side
            far_copies.append(
                copy(rows_of(2, side * 128 + k * high, high), held, far_send.at[index], far_recv.at[index], to)
            )
            relays.append(copy(held, landing, relay_send.at[index], relay_recv.at[index], to))
    near_copies = []
    for k in range(PARTS):
        part_rows = pl.ds(k * 64, 64)
        near_copies += [
            copy(rows_of(1, k * 64, 64), heads.at[3, part_rows], near_send.at[2 * k], near_recv.at[2 * k], up),
            copy(rows_of(3, k * 64, 64), heads.at[1, part_rows], near_send.at[2 * k + 1], near_recv.at[2 * k + 1], down),
        ]

    def piece_of(n):
        away = (n + 1) // 2
        odd = n % 2
        return lax.rem(z_lo + odd * (8 - away) + (1 - odd) * away, 8)

    def window(piece, n, upward):
        if upward:
            start, to = 1 + lax.div(z_lo, 7), device(x, y, z + 1, core)
        else:
            start, to = 1 - lax.div(7 - z_lo, 7), device(x, y, z - 1, core)
        return copy(
            wall.at[mine, piece, pl.ds(start, 3)], wall.at[mine, piece, pl.ds(1, 3)],
            win_send.at[n - 1], win_recv.at[n - 1], to,
        )

    def plane(n, piece, a, b, to_a, to_b, which):
        first_x = 1 - n % 2
        sx, sy = a * first_x + b * (1 - first_x), b * first_x + a * (1 - first_x)
        tx, ty = to_a * first_x + to_b * (1 - first_x), to_b * first_x + to_a * (1 - first_x)
        block = lax.rem(y + sy + 4, 4) * 4 + lax.rem(x + sx + 4, 4)
        part = wall.at[block, piece, pl.ds(1, 3)]
        index = n * 15 + which
        return copy(part, part, plane_send.at[index], plane_recv.at[index], device(x + tx, y + ty, z, core))

    def spread(n, piece, i):
        plane(n, piece, OFFSETS[i], 0, 0, 1, 3 + 3 * i).start()
        plane(n, piece, OFFSETS[i], 0, 0, -1, 4 + 3 * i).start()

    def arrive(n, which):
        part = wall.at[mine, 0, pl.ds(1, 3)]
        index = n * 15 + which
        copy(part, part, plane_send.at[index], plane_recv.at[index], sibling).wait_recv()

    def window_take(n, upward):
        piece = piece_of(n)
        window(piece, n, upward).wait_recv()

        if n + 2 < PIECES:
            window(piece, n + 2, upward).start()

        stage0(n)

    def stage0(n):
        piece = piece_of(n)
        plane(n, piece, 0, 0, 1, 0, 0).start()
        plane(n, piece, 0, 0, -1, 0, 1).start()
        spread(n, piece, 0)

    def stage1(n):
        piece = piece_of(n)
        route = lax.rem(lax.div(n, 2), 2)
        arrive(n, 0)

        @pl.when(route == 0)
        def _():
            plane(n, piece, -1, 0, 1, 0, 2).start()

        spread(n, piece, 1)
        arrive(n, 1)

        @pl.when(route == 1)
        def _():
            plane(n, piece, 1, 0, -1, 0, 2).start()

        spread(n, piece, 2)

    def stage2(n):
        piece = piece_of(n)
        arrive(n, 2)
        spread(n, piece, 3)

    def stage3(n, i):
        piece = piece_of(n)
        arrive(n, 3 + 3 * i)
        if i % 2 == 0:
            plane(n, piece, OFFSETS[i], -1, 0, 1, 5 + 3 * i).start()
        arrive(n, 4 + 3 * i)
        if i % 2 == 1:
            plane(n, piece, OFFSETS[i], 1, 0, -1, 5 + 3 * i).start()

    z_copies = [
        copy(zsum.at[step], ztake.at[step], z_send.at[step], z_recv.at[step], device(x, y, z_partner(step), core))
        for step in range(3)
    ]
    grad_copies = []
    for j in range(1, 16):
        grad_copies.append(
            copy(
                zsum.at[3], grad.at[mine], grad_send.at[j - 1], grad_recv.at[j - 1],
                device(x + j % 4, y + j // 4, z, core),
            )
        )

    def attn_step(m):
        for k in range(PARTS):
            if m == FAR_STEPS[k]:
                far_copies[2 * k].start()
                far_copies[2 * k + 1].start()
        for k in range(PARTS):
            if m == NEAR_STEPS[k]:
                near_copies[2 * k].start()
                near_copies[2 * k + 1].start()

    def sum_step(step):
        z_copies[step].wait_recv()
        zsum[step + 1] = zsum[step] + ztake[step]
        if step < 2:
            z_copies[step + 1].start()
        else:
            grad[mine] = zsum[3]
            for one in grad_copies:
                one.start()

    attn_step(0)
    for one in diff_copies:
        one.wait_recv()
    total = diff[mine].astype(jnp.float32)
    for j in range(15):
        total = total + diffs[j].astype(jnp.float32)
    zsum[0] = total
    z_copies[0].start()
    for one in firsts:
        one.wait_recv()
    second.start()
    sum_step(0)
    locals_[0].wait()
    locals_[1].wait()
    second.wait_recv()
    window(z_lo, 1, True).start()
    window(z_lo, 2, False).start()
    stage0(0)
    sum_step(1)
    attn_step(1)
    locals_[2].wait()
    locals_[3].wait()

    @pl.loop(0, BLOCKS, unroll=UNROLL)
    def _(block):
        at = pl.ds(pl.multiple_of(block * COLS, COLS), COLS)
        acc[block] = jnp.dot(
            heads[0], own[:, :, at].reshape(PIECES * ROWS, COLS), preferred_element_type=jnp.float32
        )

    for step in range(3):
        window_take(2 * step + 1, True)
        window_take(2 * step + 2, False)
        if step == 0:
            sum_step(2)
        attn_step(2 + step)
    window_take(7, True)
    attn_step(5)

    @pl.loop(0, ROUNDS)
    def _(m):
        @pl.when(m < PIECES)
        def _():
            stage1(m)
            stage3(m, 0)

        @pl.when((m >= 1) & (m < PIECES + 1))
        def _():
            stage2(m - 1)
            stage3(m - 1, 1)
            stage3(m - 1, 2)

        @pl.when(m >= 2)
        def _():
            stage3(m - 2, 3)

        for k in range(PARTS):
            if NEAR_STEPS[k] >= 6:

                @pl.when(m == NEAR_STEPS[k] - 6)
                def _(k=k):
                    near_copies[2 * k].start()
                    near_copies[2 * k + 1].start()

            @pl.when(m == RELAY_ROUNDS[k])
            def _(k=k):
                for index in (2 * k, 2 * k + 1):
                    far_copies[index].wait_recv()
                    relays[index].start()

    @pl.loop(0, PIECES)
    def _(n):
        for i in range(4):
            arrive(n, 5 + 3 * i)

    @pl.loop(0, PIECES * 15)
    def _(index):
        part_ = wall.at[mine, 0, pl.ds(1, 3)]
        copy(part_, part_, plane_send.at[index], plane_recv.at[index], sibling).wait_send()

    for n in range(1, 8):
        window(0, n, True).wait_send()
    for one in firsts + [second] + diff_copies + far_copies + z_copies:
        one.wait_send()

    for one in grad_copies:
        one.wait()

    @pl.loop(0, BLOCKS)
    def _(block):
        at = pl.ds(pl.multiple_of(block * COLS, COLS), COLS)
        summed[:, at] = grad[block, 0:12, :]

    def part(index, block):
        return jnp.dot(
            heads[index], wall[block, :, index].reshape(PIECES * ROWS, COLS), preferred_element_type=jnp.float32
        )

    for one in near_copies:
        one.wait_recv()

    for one in relays:
        one.wait_recv()
    kept = pl.ds(pl.multiple_of(core * 128, 128), 128)
    given = pl.ds(pl.multiple_of((1 - core) * 128, 128), 128)

    def half(block):
        return copy(give.at[block], take.at[block], half_send.at[block], half_recv.at[block], sibling)

    @pl.loop(0, BLOCKS, unroll=UNROLL)
    def _(block):
        acc[block] += part(1, block) + part(2, block) + part(3, block)
        give[block] = acc[block, given, :].astype(jnp.bfloat16)
        half(block).start()

    @pl.loop(0, BLOCKS, unroll=UNROLL)
    def _(block):
        at = pl.ds(pl.multiple_of(block * COLS, COLS), COLS)
        half(block).wait_recv()
        out[:, at] = (acc[block, kept, :] + take[block].astype(jnp.float32)).astype(jnp.bfloat16)

    @pl.loop(0, BLOCKS)
    def _(block):
        half(block).wait_send()

    for one in near_copies + relays:
        one.wait_send()


def local(attn_out, w_out, local_params, base_params, moment):
    vmem, hbm = pl.BlockSpec(memory_space=pltpu.VMEM), pl.BlockSpec(memory_space=pl.ANY)
    dma = pltpu.SemaphoreType.DMA
    bf16, f32 = jnp.bfloat16, jnp.float32
    projected, summed = pl.pallas_call(
        kernel,
        out_shape=(jax.ShapeDtypeStruct((128, 4096), bf16), jax.ShapeDtypeStruct((12, 4096), f32)),
        in_specs=[hbm, hbm, hbm, hbm],
        out_specs=(vmem, vmem),
        scratch_shapes=[
            pltpu.VMEM((12, 4096), bf16),
            pltpu.VMEM((12, 4096), bf16),
            pltpu.VMEM((BLOCKS, PIECES, 5, ROWS, COLS), bf16),
            pltpu.VMEM((PIECES, ROWS, 4096), bf16),
            pltpu.VMEM((4, 256, 384), bf16),
            pltpu.VMEM((2, 128, 384), bf16),
            pltpu.VMEM((BLOCKS, 256, COLS), f32),
            pltpu.VMEM((BLOCKS, 128, COLS), bf16),
            pltpu.VMEM((BLOCKS, 128, COLS), bf16),
            pltpu.VMEM((BLOCKS, 16, COLS), bf16),
            pltpu.VMEM((15, 16, COLS), bf16),
            pltpu.VMEM((4, 16, COLS), f32),
            pltpu.VMEM((3, 16, COLS), f32),
            pltpu.VMEM((BLOCKS, 16, COLS), f32),
            dma((6,)),
            dma((3,)),
            dma((3,)),
            dma((7,)),
            dma((7,)),
            dma((PIECES * 15,)),
            dma((PIECES * 15,)),
            dma((2 * PARTS,)),
            dma((2 * PARTS,)),
            dma((2 * PARTS,)),
            dma((2 * PARTS,)),
            dma((2 * PARTS,)),
            dma((2 * PARTS,)),
            dma((15,)),
            dma((15,)),
            dma((3,)),
            dma((3,)),
            dma((15,)),
            dma((15,)),
            dma((BLOCKS,)),
            dma((BLOCKS,)),
        ],
        compiler_params=pltpu.CompilerParams(
            collective_id=0, has_side_effects=True, vmem_limit_bytes=56 * 1024 * 1024
        ),
        cost_estimate=pl.CostEstimate(flops=2 * 256 * 1536 * 4096, bytes_accessed=8 << 20, transcendentals=0),
    )(attn_out, w_out.reshape(PIECES, ROWS, 4096), local_params.reshape(12, 4096), base_params)
    outer_grad = summed / lax.axis_size("replica")
    new_moment = moment_coef * moment + outer_grad
    new_params = (base_params.astype(f32) - outer_lr * (outer_grad + moment_coef * new_moment)).astype(bf16)
    return projected, new_params, new_moment


def solution(mesh):
    in_specs = (
        P("replica", "tensor"),
        P("tensor", None),
        P("replica", "tensor", None),
        P("tensor", None),
        P("tensor", None),
    )
    out_specs = (P(("replica", "tensor"), None), P("tensor", None), P("tensor", None))
    return jax.shard_map(local, mesh=mesh, in_specs=in_specs, out_specs=out_specs, check_vma=False)
```
